512 devices in a mesh: gx: 32 (over y, z_lo), ta: 16 (over z_hi, x, core).
Axes of the slice: x: 4, y: 4, z: 16 (z_hi: 2, z_lo: 8; z = z_hi * 8 + z_lo), core: 2. Of those that a mesh axis runs over, the one named last changes fastest.
Arguments:
- fields: float32 [5, 256, 512, 128], P(None, 'gx', 'ta'), may hold values from -6 to 6
- mean_axial: float32 [256, 128], P('gx'), may hold values from 0.1 to 0.9
- cycle_mean_density: float32 [128], replicated, may hold values from 0.6 to 1.4
- pml_layer: int32 [256, 128], P('gx'), may hold values from 0 to 12, as said below
- cycle_cutoff: int32 [16], replicated, may hold values from 1 to 64, as said below
Outputs:
- advanced: float32 [5, 256, 512, 128], P(None, 'gx', 'ta')
The draws below stay inside these ranges and needn't reach their ends.
Inputs may be any that keep to these rules, and one draw needn't show every extreme that they name: The last entry of cycle_cutoff is 64. pml_layer is 0 in the interior and rises towards both axial ends and the outer radius, reaching 12 at the outermost cells.
All inputs are finite; a program needn't handle non-finite values.
Results may differ from the reference program's by a relative error of at most 0.00005.
Values sent between devices are 32-bit elements; how exact they have to be, the bound alone decides.
A program may use at most 64 MiB of HBM per device.

```python
import math
import jax
import jax.numpy as jnp
from jax import lax

NR = 128
NF = 16
PMLW = 12
NX = 256
NT = 512
CMAX = 64


def draw_pml_layer(key, part):
    key_x = jax.random.fold_in(key, 11)
    key_r = jax.random.fold_in(key, 12)
    thick_x = jax.random.randint(key_x, (NR,), PMLW // 2, PMLW + 1).astype(jnp.int32)
    thick_r = jax.random.randint(key_r, (NX,), PMLW // 2, PMLW + 1).astype(jnp.int32)
    xindex = jnp.arange(NX, dtype=jnp.int32)
    rindex = jnp.arange(NR, dtype=jnp.int32)
    dist_x = jnp.minimum(xindex, NX - 1 - xindex)
    dist_r = NR - 1 - rindex
    depth_x = jnp.maximum(0, thick_x[None, :] - dist_x[:, None]) * PMLW // thick_x[None, :]
    depth_r = jnp.maximum(0, thick_r[:, None] - dist_r[None, :]) * PMLW // thick_r[:, None]
    return jnp.maximum(depth_x, depth_r).astype(jnp.int32)


def draw_cycle_cutoff(key, part):
    values = jax.random.randint(jax.random.fold_in(key, 21), (NF,), 1, CMAX + 1)
    return values.at[NF - 1].set(CMAX).astype(jnp.int32)


def steps_of(stream_key, shape, split, low, high):
    def one(position, blocks):
        heights = jax.random.uniform(jax.random.fold_in(jax.random.fold_in(stream_key, 6), position), (blocks,), jnp.float32, low / len(split), high / len(split))
        return jnp.repeat(jnp.exp(heights), shape[position] // blocks).reshape((-1,) + (1,) * (len(shape) - position - 1))

    gain = one(*split[0])
    for cut in split[1:]:
        gain = gain * one(*cut)
    return gain


def centred(own_key, dims, deviation, bound, split=(), kind=jnp.bfloat16):
    result = jax.random.normal(own_key, dims, jnp.float32) * deviation
    if len(split) > 0:
        result = steps_of(own_key, dims, split, -0.22, 0.18) * result
    return jnp.clip(result, min=-bound, max=bound).astype(kind)


def setup_inputs(seed: int = 0) -> dict:
    arg_keys = jax.random.split(jax.random.key(seed), 6)
    return {
        "fields": centred(arg_keys[0], (5, NX, NT, NR), 1.0, 6.0, ((1, 32), (2, 16)), jnp.float32),
        "mean_axial": jnp.clip(0.1 + 0.79999997 * jax.random.uniform(arg_keys[1], (NX, NR), jnp.float32) ** steps_of(arg_keys[1], (NX, NR), ((0, 32),), -0.2, 0.2), 0.1, 0.9),
        "cycle_mean_density": jnp.clip(jax.random.uniform(arg_keys[2], (NR,), jnp.float32, 0.6, 1.4), 0.6, 1.4),
        "pml_layer": draw_pml_layer(jax.random.fold_in(arg_keys[5], 71), 0),
        "cycle_cutoff": draw_cycle_cutoff(jax.random.fold_in(arg_keys[5], 71), 0),
    }


coefs = (0.770882380518, -0.166705904415, 0.020843142770)
time_step = 0.1
damping_peak = 4.0


def derive(extended, axis, count):
    total = jnp.zeros_like(lax.slice_in_dim(extended, 3, 3 + count, axis=axis))
    for shift, weight in enumerate(coefs, 1):
        upper = lax.slice_in_dim(extended, 3 + shift, 3 + shift + count, axis=axis)
        lower = lax.slice_in_dim(extended, 3 - shift, 3 - shift + count, axis=axis)
        total = total + weight * (upper - lower)
    return total


def advance(fields, ext_x, ext_t, partner, mean_axial, cycle_mean_density, pml_layer, angular_spacing):
    flips = jnp.array([1.0, 1.0, -1.0, -1.0, 1.0], jnp.float32).reshape(5, 1, 1, 1)
    ghost = (partner * flips)[..., ::-1]
    outside = jnp.zeros(fields.shape[:3] + (3,), jnp.float32)
    ext_r = jnp.concatenate([ghost, fields, outside], axis=3)
    axial_derivative_step = derive(ext_x, 1, fields.shape[1])
    angular_derivative_step = derive(ext_t, 2, fields.shape[2])
    radial_derivative_step = derive(ext_r, 3, fields.shape[3])
    radius = jnp.arange(fields.shape[3], dtype=jnp.float32) + 0.5
    inverse_radius = 1.0 / radius
    axial = mean_axial[:, None, :]
    density_field = cycle_mean_density
    dilatation = axial_derivative_step[1] + radial_derivative_step[2] + fields[2] * inverse_radius + angular_derivative_step[3] * (inverse_radius / angular_spacing)
    convection_term = axial * axial_derivative_step
    density_rate = -(convection_term[0] + density_field * dilatation)
    rate_u = -(convection_term[1] + axial_derivative_step[4] / density_field)
    rate_v = -(convection_term[2] + radial_derivative_step[4] / density_field)
    rate_w = -(convection_term[3] + angular_derivative_step[4] * inverse_radius / (density_field * angular_spacing))
    pressure_rate = -(convection_term[4] + dilatation)
    rate = jnp.stack([density_rate, rate_u, rate_v, rate_w, pressure_rate])
    depth = pml_layer.astype(jnp.float32) / PMLW
    sigma = (damping_peak * depth * depth)[:, None, :]
    return fields + time_step * (rate - sigma * fields)


def reference(fields, mean_axial, cycle_mean_density, pml_layer, cycle_cutoff):
    n_theta = fields.shape[2]
    ext_x = jnp.pad(fields, ((0, 0), (3, 3), (0, 0), (0, 0)))
    ext_t = jnp.concatenate([fields[:, :, -3:], fields, fields[:, :, :3]], axis=2)
    partner = jnp.roll(fields[..., :3], n_theta // 2, axis=2)
    stepped = advance(fields, ext_x, ext_t, partner, mean_axial, cycle_mean_density, pml_layer, 2.0 * math.pi / n_theta)
    inner = stepped[..., :NF]
    spectrum = jnp.fft.rfft(inner, axis=2)
    modes = jnp.arange(n_theta // 2 + 1, dtype=jnp.int32)
    keep = (modes[:, None] <= cycle_cutoff[None, :])
    spectrum = jnp.where(keep, spectrum, jnp.zeros_like(spectrum))
    filtered = jnp.fft.irfft(spectrum, n=n_theta, axis=2).astype(jnp.float32)
    return jnp.concatenate([filtered, stepped[..., NF:]], axis=3)
```

```python
import functools
import math

import jax
import jax.numpy as jnp
import numpy as np
from jax import lax
from jax.experimental import pallas as pl
from jax.experimental.pallas import tpu as pltpu
from jax.sharding import PartitionSpec as P

NF = 16
PMLW = 12
MODES = 64
LANES = 128

A1, A2, A3 = 0.770882380518, -0.166705904415, 0.020843142770
DT = 0.1
PEAK = 4.0
F32 = jnp.float32
MESH = pl.DeviceIdType.MESH


def left(x, by):
    return pltpu.roll(x, LANES - by, x.ndim - 1)


def right(x, by):
    return pltpu.roll(x, by, x.ndim - 1)


def periodic(x, lane):
    x = jnp.where(lane < NF, x, 0.0)
    x = x + right(x, 16)
    x = x + right(x, 32)
    return x + right(x, 64)


def group(lane, g):
    return (lane >= NF * g) & (lane < NF * (g + 1))


def body(
    n_gx, n_ta, spacing,
    fields, mean, dens, pml, cut, forward, inverse, out,
    fx, ext, rx, ex, zr, dp, qs, gr, th_out, th_in, ps, pr, bs, br, mt, st, sg,
    load_sem, ring_send, ring_recv, th_send, th_recv, rx_send, rx_recv,
    a_send, a_recv, z_send, z_recv, b_send, b_recv,
):
    half = n_ta // 2
    gx = lax.axis_index("gx")
    ta = lax.axis_index("ta")
    k = lax.rem(ta, half)
    base = ta - k
    partner = lax.rem(ta + half, n_ta)
    after = lax.rem(ta + 1, n_ta)
    before = lax.rem(ta + n_ta - 1, n_ta)
    has_low = gx > 0
    has_high = gx < n_gx - 1
    low = jnp.maximum(gx - 1, 0)
    high = jnp.minimum(gx + 1, n_gx - 1)
    edge_low = k == 0
    edge_high = k == half - 1
    mates = [base + lax.rem(k + i, half) for i in range(1, half)]

    barrier = pltpu.get_barrier_semaphore()

    def greet(**where):
        pl.semaphore_signal(barrier, inc=1, device_id=where, device_id_type=MESH)

    for mate in mates:
        greet(ta=mate)
    greet(ta=partner)
    pl.when(has_low)(lambda: greet(gx=low))
    pl.when(has_high)(lambda: greet(gx=high))
    pl.when(edge_low)(lambda: greet(ta=before))
    pl.when(edge_high)(lambda: greet(ta=after))

    load = pltpu.make_async_copy(fields, fx.at[:, 3:11], load_sem.at[0])
    load.start()
    load_t = pltpu.make_async_copy(fields.at[3:5], ext.at[:, :, 8:40], load_sem.at[1])
    load_t.start()

    lane = lax.broadcasted_iota(jnp.int32, (1, LANES), 1)
    lane8 = lax.broadcasted_iota(jnp.int32, (8, LANES), 1)
    inv_r = 1.0 / (lane.astype(F32) + 0.5)
    inv_dt = 1.0 / spacing
    rho0 = dens[...]
    depth = pml[...].astype(F32) / PMLW
    damp = 1.0 - DT * (PEAK * depth * depth)
    st[...] = damp
    mt[...] = periodic(mean[...], lane8)
    sg[...] = periodic(damp, lane8)
    rho0_p = periodic(jnp.broadcast_to(rho0, (8, LANES)), lane8)[0:1]
    inv_r_p = periodic(jnp.broadcast_to(inv_r, (8, LANES)), lane8)[0:1]

    def on(g, value):
        return jnp.where(group(lane, g), value, 0.0)

    up_w = [jnp.where(lane < LANES - s, a, 0.0) for s, a in ((1, A1), (2, A2), (3, A3))]
    dn_w = [jnp.where(lane >= s, a, 0.0) for s, a in ((1, A1), (2, A2), (3, A3))]
    g_0 = jnp.where(lane == 0, A1, jnp.where(lane == 1, A3, 0.0))
    g_u1 = jnp.where(lane == 0, A2, 0.0)
    g_u2 = jnp.where(lane == 0, A3, 0.0)
    g_d1 = jnp.where(lane == 1, A2, 0.0)
    g_d2 = jnp.where(lane == 2, A3, 0.0)
    c_e = on(0, -DT * rho0_p) + on(2, -DT / rho0_p) + on(4, -DT)

    def radial(f):
        ups = [left(f, s) for s in (1, 2, 3)]
        dns = [right(f, s) for s in (1, 2, 3)]
        d = (up_w[0] * ups[0] - dn_w[0] * dns[0]) + (up_w[1] * ups[1] - dn_w[1] * dns[1])
        d = d + (up_w[2] * ups[2] - dn_w[2] * dns[2])
        ghost = g_0 * f + g_u1 * ups[0] + g_u2 * ups[1] + g_d1 * dns[0] + g_d2 * dns[1]
        return d, ghost

    load.wait()
    load_t.wait()

    def pack(x, carry):
        rho, u, v, w, p = (fx[f, 3 + x] for f in range(5))
        dv, gv = radial(v)
        dpr, gp = radial(p)
        z = dv + v * inv_r
        zr[x] = z
        dp[x] = dpr
        r = jnp.where(lane < 96, right(w, 80), jnp.where(lane < 112, right(p, 96), right(gv, 112) + right(gp, 115)))
        r = jnp.where(lane < 80, right(p, 64), r)
        r = jnp.where(lane < 64, right(w, 48), r)
        r = jnp.where(lane < 48, right(v, 32), r)
        r = jnp.where(lane < 32, right(u, 16), r)
        r = jnp.where(lane < 16, rho, r)
        rx[3 + x] = r
        e = jnp.where(lane < 16, z, jnp.where(lane < 48, right(dpr, 32), right(z, 64)))
        ex[x] = e * c_e
        for f in range(2):
            th_out[0, x, 3 * f : 3 * f + 3] = ext[f, x, 8:11]
            th_out[1, x, 3 * f : 3 * f + 3] = ext[f, x, 37:40]
        return carry

    th_out[...] = jnp.zeros_like(th_out)
    lax.fori_loop(0, 8, pack, 0)

    pl.semaphore_wait(
        barrier,
        half + has_low.astype(jnp.int32) + has_high.astype(jnp.int32) + edge_low.astype(jnp.int32) + edge_high.astype(jnp.int32),
    )

    def remote(src, dst, send, recv, **where):
        return pltpu.make_async_remote_copy(
            src_ref=src, dst_ref=dst, send_sem=send, recv_sem=recv, device_id=where, device_id_type=MESH
        )

    rx_up = remote(rx.at[8:11], rx.at[0:3], rx_send.at[0], rx_recv.at[0], gx=high)
    rx_down = remote(rx.at[3:6], rx.at[11:14], rx_send.at[1], rx_recv.at[1], gx=low)
    fx_up = remote(fx.at[:, 8:11], fx.at[:, 0:3], ring_send.at[0], ring_recv.at[0], gx=high)
    fx_down = remote(fx.at[:, 3:6], fx.at[:, 11:14], ring_send.at[1], ring_recv.at[1], gx=low)
    th_down = remote(th_out.at[0], th_in.at[1], th_send.at[0], th_recv.at[1], ta=before)
    th_up = remote(th_out.at[1], th_in.at[0], th_send.at[1], th_recv.at[0], ta=after)

    pl.when(has_high)(rx_up.start)
    pl.when(has_low)(rx_down.start)
    th_down.start()
    th_up.start()
    pl.when(has_high)(fx_up.start)
    pl.when(has_low)(fx_down.start)

    @pl.when(jnp.logical_not(has_low))
    def _():
        rx[0:3] = jnp.zeros((3,) + rx.shape[1:], F32)
        fx[:, 0:3] = jnp.zeros((5, 3) + fx.shape[2:], F32)

    @pl.when(jnp.logical_not(has_high))
    def _():
        rx[11:14] = jnp.zeros((3,) + rx.shape[1:], F32)
        fx[:, 11:14] = jnp.zeros((5, 3) + fx.shape[2:], F32)

    c_a = on(0, -DT * rho0_p)
    c_b = on(1, -DT / rho0_p)
    c_c = on(4, -DT)

    pl.when(has_low)(rx_up.wait_recv)
    pl.when(has_high)(rx_down.wait_recv)

    def step_inner(x, carry):
        d = A1 * (rx[4 + x] - rx[2 + x]) + A2 * (rx[5 + x] - rx[1 + x]) + A3 * (rx[6 + x] - rx[x])
        r = rx[3 + x]
        row = pl.ds(x, 1)
        s = r * sg[row] - (DT * mt[row]) * d + ex[x]
        s = s + c_a * left(d, 16) + c_b * left(d, 48) + c_c * right(d, 48)
        qs[x] = jnp.where(lane < 80, s, r)
        return carry

    lax.fori_loop(0, 8, step_inner, 0)

    a_copies = []
    for i in range(1, half):
        there = lax.rem(k + i, half)
        copy = remote(qs.at[there], gr.at[k], a_send.at[i - 1], a_recv.at[i - 1], ta=base + there)
        copy.start()
        a_copies.append(copy)
    gr[k] = qs[k]

    th_up.wait_recv()
    th_down.wait_recv()
    damp_rho = -DT * rho0
    damp_v = -DT / rho0

    def local_part(x, carry):
        for f in range(2):
            ext[f, x, 5:8] = th_in[0, x, 3 * f : 3 * f + 3]
            ext[f, x, 40:43] = th_in[1, x, 3 * f : 3 * f + 3]

        def angular(f):
            d = A1 * (ext[f, x, 9:41] - ext[f, x, 7:39]) + A2 * (ext[f, x, 10:42] - ext[f, x, 6:38])
            return d + A3 * (ext[f, x, 11:43] - ext[f, x, 5:37])

        keep = st[pl.ds(x, 1)]
        around = inv_r * inv_dt
        z = zr[x] + angular(0) * around
        out[0, x] = fx[0, 3 + x] * keep + damp_rho * z
        out[1, x] = fx[1, 3 + x] * keep
        out[2, x] = fx[2, 3 + x] * keep + damp_v * dp[x]
        out[3, x] = fx[3, 3 + x] * keep + damp_v * (angular(1) * around)
        out[4, x] = fx[4, 3 + x] * keep - DT * z
        return carry

    lax.fori_loop(0, 8, local_part, 0)

    for copy in a_copies:
        copy.wait()
    g = gr[...].reshape(8 * gr.shape[1], LANES)
    highest = lax.Precision.HIGHEST
    coef = jnp.dot(forward[...], g, precision=highest, preferred_element_type=F32)
    zero_mode = jnp.sum(g, axis=0, keepdims=True)
    a_m, b_m = coef[:MODES], coef[MODES:]
    kappa = 2.0 * (A1 * forward[MODES:, 1:2] + A2 * forward[MODES:, 2:3] + A3 * forward[MODES:, 3:4])
    row = lax.broadcasted_iota(jnp.int32, (MODES, LANES), 0)
    sign = jnp.where(lax.rem(row, 2) == 1, 1.0, -1.0)
    around_p = -DT * inv_r_p * inv_dt
    t_r, t_p, t_w = on(0, around_p * rho0_p), on(4, around_p), on(3, around_p / rho0_p)
    three = lane < 3
    h_r = jnp.where(three, -DT * rho0_p, 0.0)
    h_p = jnp.where((lane >= 64) & (lane < 67), -DT, 0.0)
    h_v = jnp.where((lane >= 32) & (lane < 35), DT / rho0_p, 0.0)

    def turned(c):
        return t_r * left(c, 80) + t_p * left(c, 16) + t_w * left(c, 48)

    def mirrored(c):
        return h_r * left(c, 112) + h_p * left(c, 48) + h_v * left(c, 83)

    new_a = a_m + turned(kappa * b_m) + sign * mirrored(a_m)
    new_b = b_m - turned(kappa * a_m) + sign * mirrored(b_m)
    zero8 = jnp.broadcast_to(zero_mode, (8, LANES))
    zero8 = zero8 + mirrored(zero8)

    for h, c in ((0, new_a), (1, new_b)):
        t5, t6, t7 = c[40:48], c[48:56], c[56:64]
        for i in range(5):
            spread = jnp.where(lane < 112, right(t6, 96 - 16 * i), right(t7, 112 - 16 * i))
            spread = jnp.where(lane < 96, right(t5, 80 - 16 * i), spread)
            ps[5 * h + i] = jnp.where(lane < 80, c[8 * i : 8 * i + 8], spread)
    ps[10] = zero8
    across = remote(ps, pr, z_send, z_recv, ta=partner)
    across.start()
    cuts = jnp.concatenate([cut[...]] * 8, axis=1)
    keep = jnp.where(row + 1 <= cuts, 2.0 / (n_ta * gr.shape[1]), 0.0)
    across.wait()

    total = []
    for h, c in ((0, new_a), (1, new_b)):
        parts = [pr[5 * h + i] for i in range(5)]
        tiles = list(parts)
        for first in (80, 96, 112):
            tile = left(parts[0], first)
            for i in range(1, 5):
                tile = jnp.where(lane < 16 * i, tile, left(parts[i], first - 16 * i))
            tiles.append(tile)
        total.append((c + sign * jnp.concatenate(tiles, axis=0)) * keep)
    both = jnp.concatenate(total, axis=0)
    mean_mode = (zero8 + pr[10])[0:1] * (1.0 / (n_ta * gr.shape[1]))
    filtered = jnp.dot(inverse[...], both, precision=highest, preferred_element_type=F32) + mean_mode
    bs[...] = filtered.reshape(bs.shape)

    b_copies = []
    for i in range(1, half):
        there = lax.rem(k + i, half)
        copy = remote(bs.at[there], br.at[k], b_send.at[i - 1], b_recv.at[i - 1], ta=base + there)
        copy.start()
        b_copies.append(copy)
    br[k] = bs[k]

    pl.when(has_low)(fx_up.wait_recv)
    pl.when(has_high)(fx_down.wait_recv)
    inv_rho0 = 1.0 / rho0

    def axial_part(x, carry):
        def axial(f):
            d = A1 * (fx[f, 4 + x] - fx[f, 2 + x]) + A2 * (fx[f, 5 + x] - fx[f, 1 + x])
            return d + A3 * (fx[f, 6 + x] - fx[f, x])

        along = DT * mean[pl.ds(x, 1)]
        d_u, d_p = axial(1), axial(4)
        out[0, x] = out[0, x] - along * axial(0) + damp_rho * d_u
        out[1, x] = out[1, x] - along * d_u + damp_v * d_p
        out[2, x] = out[2, x] - along * axial(2)
        out[3, x] = out[3, x] - along * axial(3)
        out[4, x] = out[4, x] - along * d_p - DT * d_u
        return carry

    lax.fori_loop(0, 8, axial_part, 0)

    for copy in b_copies:
        copy.wait()

    def merge(x, carry):
        t = br[x]
        for f in range(5):
            out[f, x] = jnp.where(lane < NF, left(t, 16 * f) if f else t, out[f, x])
        return carry

    lax.fori_loop(0, 8, merge, 0)

    pl.when(has_high)(rx_up.wait_send)
    pl.when(has_low)(rx_down.wait_send)
    pl.when(has_high)(fx_up.wait_send)
    pl.when(has_low)(fx_down.wait_send)
    th_down.wait_send()
    th_up.wait_send()


def tables(points, n_theta):
    n = np.arange(points)
    m = np.arange(1, MODES + 1)
    phase = (m[:, None] * n[None, :] % n_theta) * (2.0 * math.pi / n_theta)
    forward = np.concatenate([np.cos(phase), np.sin(phase)]).astype(np.float32)
    return forward, np.ascontiguousarray(forward.T)


def solution(mesh):
    n_gx, n_ta = mesh.shape["gx"], mesh.shape["ta"]

    def on_device(fields, mean_axial, cycle_mean_density, pml_layer, cycle_cutoff):
        nf, nx, nt, nr = fields.shape
        n_theta = nt * n_ta
        forward, inverse = tables(n_theta // 2, n_theta)
        vmem = pl.BlockSpec(memory_space=pltpu.VMEM)
        half = n_ta // 2
        dma = pltpu.SemaphoreType.DMA
        return pl.pallas_call(
            functools.partial(body, n_gx, n_ta, 2.0 * math.pi / n_theta),
            out_shape=jax.ShapeDtypeStruct(fields.shape, F32),
            in_specs=[pl.BlockSpec(memory_space=pl.ANY)] + [vmem] * 6,
            out_specs=vmem,
            scratch_shapes=[
                pltpu.VMEM((nf, nx + 6, nt, nr), F32),
                pltpu.VMEM((2, nx, nt + 16, nr), F32),
                pltpu.VMEM((nx + 6, nt, nr), F32),
                pltpu.VMEM((nx, nt, nr), F32),
                pltpu.VMEM((nx, nt, nr), F32),
                pltpu.VMEM((nx, nt, nr), F32),
                pltpu.VMEM((nx, nt, nr), F32),
                pltpu.VMEM((nx, nt, nr), F32),
                pltpu.VMEM((2, nx, 8, nr), F32),
                pltpu.VMEM((2, nx, 8, nr), F32),
                pltpu.VMEM((11, 8, nr), F32),
                pltpu.VMEM((11, 8, nr), F32),
                pltpu.VMEM((nx, nt, nr), F32),
                pltpu.VMEM((nx, nt, nr), F32),
                pltpu.VMEM((nx, nr), F32),
                pltpu.VMEM((nx, nr), F32),
                pltpu.VMEM((nx, nr), F32),
                dma((2,)),
                dma((2,)), dma((2,)),
                dma((2,)), dma((2,)),
                dma((2,)), dma((2,)),
                dma((half - 1,)), dma((half - 1,)),
                dma, dma,
                dma((half - 1,)), dma((half - 1,)),
            ],
            compiler_params=pltpu.CompilerParams(
                collective_id=0, has_side_effects=True, vmem_limit_bytes=16 * 1024 * 1024
            ),
        )(
            fields,
            mean_axial,
            cycle_mean_density.reshape(1, nr),
            pml_layer,
            cycle_cutoff.reshape(1, NF),
            jnp.asarray(forward),
            jnp.asarray(inverse),
        )

    return jax.shard_map(
        on_device,
        mesh=mesh,
        in_specs=(P(None, "gx", "ta", None), P("gx", None), P(), P("gx", None), P()),
        out_specs=P(None, "gx", "ta", None),
        check_vma=False,
    )
```

```python
import functools
import math

import jax
import jax.numpy as jnp
import numpy as np
from jax import lax
from jax.experimental import pallas as pl
from jax.experimental.pallas import tpu as pltpu
from jax.sharding import PartitionSpec as P

NF = 16
PMLW = 12
MODES = 64
LANES = 128

A1, A2, A3 = 0.770882380518, -0.166705904415, 0.020843142770
DT = 0.1
PEAK = 4.0
F32 = jnp.float32
MESH = pl.DeviceIdType.MESH


def left(x, by):
    return pltpu.roll(x, LANES - by, x.ndim - 1)


def right(x, by):
    return pltpu.roll(x, by, x.ndim - 1)


def periodic(x, lane):
    x = jnp.where(lane < NF, x, 0.0)
    x = x + right(x, 16)
    x = x + right(x, 32)
    return x + right(x, 64)


def group(lane, g):
    return (lane >= NF * g) & (lane < NF * (g + 1))


def body(
    n_gx, n_ta, spacing,
    fields, *rest,
):
    inputs, rest = rest[:6], rest[6:]
    out, rest = rest[0], rest[1:]
    local, rest = rest[:6], rest[6:]
    input_sem, rest = rest[0], rest[1:]
    mean, dens, pml, cut, forward, inverse = local
    (
    fx, ext, rx, ex, zr, dp, qs, gr, hs, hr, th_out, th_in, ps, pr, bs, br, mt, st, sg,
    load_sem, ring_send, ring_recv, th_send, th_recv, h_send, h_recv,
    a_send, a_recv, z_send, z_recv, b_send, b_recv, far,
    ) = rest
    half = n_ta // 2
    gx = lax.axis_index("gx")
    ta = lax.axis_index("ta")
    k = lax.rem(ta, half)
    base = ta - k
    partner = lax.rem(ta + half, n_ta)
    after = lax.rem(ta + 1, n_ta)
    before = lax.rem(ta + n_ta - 1, n_ta)
    has_low = gx > 0
    has_high = gx < n_gx - 1
    low = jnp.maximum(gx - 1, 0)
    high = jnp.minimum(gx + 1, n_gx - 1)
    edge_low = k == 0
    edge_high = k == half - 1
    second = ta >= half
    mates = [base + lax.rem(k + i, half) for i in range(1, half)]
    takes_low = k < 3
    takes_high = k > half - 4

    barrier = pltpu.get_barrier_semaphore()

    def greet(sem, **where):
        pl.semaphore_signal(sem, inc=1, device_id=where, device_id_type=MESH)

    def greet_across(sem):
        greet(sem, ta=partner)
        pl.when(edge_low)(lambda: greet(sem, ta=before))
        pl.when(edge_high)(lambda: greet(sem, ta=after))

    for mate in mates:
        greet(barrier, ta=mate)
    pl.when(jnp.logical_not(second))(lambda: greet_across(barrier))
    for exists, takes, there in ((has_low, takes_low, low), (has_high, takes_high, high)):

        @pl.when(exists)
        def _():
            greet(barrier, gx=there)

            @pl.when(takes)
            def _():
                for mate in mates:
                    greet(barrier, gx=there, ta=mate)

    load = pltpu.make_async_copy(fields, fx.at[:, 3:11], load_sem.at[0])
    load.start()
    load_t = pltpu.make_async_copy(fields.at[3:5], ext.at[:, :, 8:40], load_sem.at[1])
    load_t.start()
    small = [pltpu.make_async_copy(inputs[i], local[i], input_sem.at[i]) for i in range(6)]
    for copy in small:
        copy.start()
    for copy in small[:4]:
        copy.wait()

    lane = lax.broadcasted_iota(jnp.int32, (1, LANES), 1)
    lane8 = lax.broadcasted_iota(jnp.int32, (8, LANES), 1)
    inv_r = 1.0 / (lane.astype(F32) + 0.5)
    inv_dt = 1.0 / spacing
    rho0 = dens[...]
    depth = pml[...].astype(F32) / PMLW
    damp = 1.0 - DT * (PEAK * depth * depth)
    st[...] = damp
    mt[...] = periodic(mean[...], lane8)
    sg[...] = periodic(damp, lane8)
    rho0_p = periodic(jnp.broadcast_to(rho0, (8, LANES)), lane8)[0:1]
    inv_r_p = periodic(jnp.broadcast_to(inv_r, (8, LANES)), lane8)[0:1]

    def on(g, value):
        return jnp.where(group(lane, g), value, 0.0)

    up_w = [jnp.where(lane < LANES - s, a, 0.0) for s, a in ((1, A1), (2, A2), (3, A3))]
    dn_w = [jnp.where(lane >= s, a, 0.0) for s, a in ((1, A1), (2, A2), (3, A3))]
    g_0 = jnp.where(lane == 0, A1, jnp.where(lane == 1, A3, 0.0))
    g_u1 = jnp.where(lane == 0, A2, 0.0)
    g_u2 = jnp.where(lane == 0, A3, 0.0)
    g_d1 = jnp.where(lane == 1, A2, 0.0)
    g_d2 = jnp.where(lane == 2, A3, 0.0)
    c_e = on(0, -DT * rho0_p) + on(2, -DT / rho0_p) + on(4, -DT)

    def radial(f):
        ups = [left(f, s) for s in (1, 2, 3)]
        dns = [right(f, s) for s in (1, 2, 3)]
        d = (up_w[0] * ups[0] - dn_w[0] * dns[0]) + (up_w[1] * ups[1] - dn_w[1] * dns[1])
        d = d + (up_w[2] * ups[2] - dn_w[2] * dns[2])
        ghost = g_0 * f + g_u1 * ups[0] + g_u2 * ups[1] + g_d1 * dns[0] + g_d2 * dns[1]
        return d, ghost

    load.wait()
    load_t.wait()

    def pack(x, carry):
        rho, u, v, w, p = (fx[f, 3 + x] for f in range(5))
        dv, gv = radial(v)
        dpr, gp = radial(p)
        z = dv + v * inv_r
        zr[x] = z
        dp[x] = dpr
        r = jnp.where(lane < 96, right(w, 80), jnp.where(lane < 112, right(p, 96), right(gv, 112) + right(gp, 115)))
        r = jnp.where(lane < 80, right(p, 64), r)
        r = jnp.where(lane < 64, right(w, 48), r)
        r = jnp.where(lane < 48, right(v, 32), r)
        r = jnp.where(lane < 32, right(u, 16), r)
        r = jnp.where(lane < 16, rho, r)
        rx[3 + x] = r
        e = jnp.where(lane < 16, z, jnp.where(lane < 48, right(dpr, 32), right(z, 64)))
        ex[x] = e * c_e
        for f in range(2):
            th_out[0, x, 3 * f : 3 * f + 3] = ext[f, x, 8:11]
            th_out[1, x, 3 * f : 3 * f + 3] = ext[f, x, 37:40]
        return carry

    th_out[...] = jnp.zeros_like(th_out)
    rx[0:3] = jnp.zeros((3,) + rx.shape[1:], F32)
    rx[11:14] = jnp.zeros((3,) + rx.shape[1:], F32)
    lax.fori_loop(0, 8, pack, 0)

    c_a = on(0, -DT * rho0_p)
    c_b = on(1, -DT / rho0_p)
    c_c = on(4, -DT)
    fields_only = lane < 5 * NF

    def advected(d, speed):
        return c_a * left(d, 16) + c_b * left(d, 48) + c_c * right(d, 48) - (DT * speed) * d

    def step_inner(x, carry):
        d = A1 * (rx[4 + x] - rx[2 + x]) + A2 * (rx[5 + x] - rx[1 + x]) + A3 * (rx[6 + x] - rx[x])
        r = rx[3 + x]
        row = pl.ds(x, 1)
        s = r * sg[row] + advected(d, mt[row]) + ex[x]
        qs[x] = jnp.where(fields_only, s, r)
        return carry

    lax.fori_loop(0, 8, step_inner, 0)
    hs[0] = -(A1 * rx[10] + A2 * rx[9] + A3 * rx[8])
    hs[1] = -(A2 * rx[10] + A3 * rx[9])
    hs[2] = -A3 * rx[10]
    hs[3] = A3 * rx[3]
    hs[4] = A2 * rx[3] + A3 * rx[4]
    hs[5] = A1 * rx[3] + A2 * rx[4] + A3 * rx[5]

    comes = (takes_low & has_low) | (takes_high & has_high)

    @pl.when(jnp.logical_not(comes))
    def _():
        hr[...] = jnp.zeros_like(hr)

    def count(flag):
        return flag.astype(jnp.int32)

    crossing = 1 + count(edge_low) + count(edge_high)
    from_low = count(has_low) * (4 - count(takes_high))
    from_high = count(has_high) * (4 - count(takes_low))
    pl.semaphore_wait(barrier, half - 1 + from_low + from_high + count(second) * crossing)
    pl.when(second)(lambda: greet_across(far))

    def remote(src, dst, send, recv, **where):
        return pltpu.make_async_remote_copy(
            src_ref=src, dst_ref=dst, send_sem=send, recv_sem=recv, device_id=where, device_id_type=MESH
        )

    h_up = [remote(hs.at[j], hr.at[k], h_send.at[j], h_recv.at[k], gx=high, ta=base + j) for j in range(3)]
    h_down = [
        remote(hs.at[j], hr.at[k], h_send.at[j], h_recv.at[k], gx=low, ta=base + half - 6 + j) for j in range(3, 6)
    ]
    fx_up = remote(fx.at[:, 8:11], fx.at[:, 0:3], ring_send.at[0], ring_recv.at[0], gx=high)
    fx_down = remote(fx.at[:, 3:6], fx.at[:, 11:14], ring_send.at[1], ring_recv.at[1], gx=low)
    th_down = remote(th_out.at[0], th_in.at[1], th_send.at[0], th_recv.at[1], ta=before)
    th_up = remote(th_out.at[1], th_in.at[0], th_send.at[1], th_recv.at[0], ta=after)

    def each(copies, method):
        for copy in copies:
            getattr(copy, method)()

    pl.when(has_high)(lambda: each(h_up, "start"))
    pl.when(has_low)(lambda: each(h_down, "start"))
    a_copies = []
    for i in range(1, half):
        there = lax.rem(k + i, half)
        copy = remote(qs.at[there], gr.at[k], a_send.at[i - 1], a_recv.at[i - 1], ta=base + there)
        copy.start()
        a_copies.append(copy)
    gr[k] = qs[k]

    pl.when(second | jnp.logical_not(edge_low))(th_down.start)
    pl.when(second | jnp.logical_not(edge_high))(th_up.start)

    def send_bulk():
        pl.when(has_high)(fx_up.start)
        pl.when(has_low)(fx_down.start)

    pl.when(jnp.logical_not(second))(send_bulk)

    @pl.when(jnp.logical_not(has_low))
    def _():
        fx[:, 0:3] = jnp.zeros((5, 3) + fx.shape[2:], F32)

    @pl.when(jnp.logical_not(has_high))
    def _():
        fx[:, 11:14] = jnp.zeros((5, 3) + fx.shape[2:], F32)

    for copy in a_copies:
        copy.wait()
    for copy in small[4:]:
        copy.wait()

    @pl.when(comes)
    def _():
        for j in range(half):
            remote(hs.at[0], hr.at[j], h_send.at[0], h_recv.at[j], gx=low).wait_recv()

    speed = jnp.where(fields_only, mt[pl.ds(k, 1)], 0.0)
    g = gr[...] + advected(hr[...], speed)
    g = g.reshape(8 * gr.shape[1], LANES)
    highest = lax.Precision.HIGHEST
    coef = jnp.dot(forward[...], g, precision=highest, preferred_element_type=F32)
    zero_mode = jnp.sum(g, axis=0, keepdims=True)
    a_m, b_m = coef[:MODES], coef[MODES:]
    kappa = 2.0 * (A1 * forward[MODES:, 1:2] + A2 * forward[MODES:, 2:3] + A3 * forward[MODES:, 3:4])
    row = lax.broadcasted_iota(jnp.int32, (MODES, LANES), 0)
    sign = jnp.where(lax.rem(row, 2) == 1, 1.0, -1.0)
    around_p = -DT * inv_r_p * inv_dt
    t_r, t_p, t_w = on(0, around_p * rho0_p), on(4, around_p), on(3, around_p / rho0_p)
    three = lane < 3
    h_r = jnp.where(three, -DT * rho0_p, 0.0)
    h_p = jnp.where((lane >= 64) & (lane < 67), -DT, 0.0)
    h_v = jnp.where((lane >= 32) & (lane < 35), DT / rho0_p, 0.0)

    def turned(c):
        return t_r * left(c, 80) + t_p * left(c, 16) + t_w * left(c, 48)

    def mirrored(c):
        return h_r * left(c, 112) + h_p * left(c, 48) + h_v * left(c, 83)

    new_a = a_m + turned(kappa * b_m) + sign * mirrored(a_m)
    new_b = b_m - turned(kappa * a_m) + sign * mirrored(b_m)
    zero8 = jnp.broadcast_to(zero_mode, (8, LANES))
    zero8 = zero8 + mirrored(zero8)

    for h, c in ((0, new_a), (1, new_b)):
        t5, t6, t7 = c[40:48], c[48:56], c[56:64]
        for i in range(5):
            spread = jnp.where(lane < 112, right(t6, 96 - 16 * i), right(t7, 112 - 16 * i))
            spread = jnp.where(lane < 96, right(t5, 80 - 16 * i), spread)
            ps[5 * h + i] = jnp.where(lane < 80, c[8 * i : 8 * i + 8], spread)
    ps[10] = zero8
    across = remote(ps, pr, z_send, z_recv, ta=partner)

    @pl.when(jnp.logical_not(second))
    def _():
        pl.semaphore_wait(far, crossing)
        pl.when(edge_low)(th_down.start)
        pl.when(edge_high)(th_up.start)

    across.start()
    pl.when(second)(send_bulk)
    th_up.wait_recv()
    th_down.wait_recv()
    damp_rho = -DT * rho0
    damp_v = -DT / rho0

    def local_part(x, carry):
        for f in range(2):
            ext[f, x, 5:8] = th_in[0, x, 3 * f : 3 * f + 3]
            ext[f, x, 40:43] = th_in[1, x, 3 * f : 3 * f + 3]

        def angular(f):
            d = A1 * (ext[f, x, 9:41] - ext[f, x, 7:39]) + A2 * (ext[f, x, 10:42] - ext[f, x, 6:38])
            return d + A3 * (ext[f, x, 11:43] - ext[f, x, 5:37])

        keep = st[pl.ds(x, 1)]
        around = inv_r * inv_dt
        z = zr[x] + angular(0) * around
        out[0, x] = fx[0, 3 + x] * keep + damp_rho * z
        out[1, x] = fx[1, 3 + x] * keep
        out[2, x] = fx[2, 3 + x] * keep + damp_v * dp[x]
        out[3, x] = fx[3, 3 + x] * keep + damp_v * (angular(1) * around)
        out[4, x] = fx[4, 3 + x] * keep - DT * z
        return carry

    lax.fori_loop(0, 8, local_part, 0)

    cuts = jnp.concatenate([cut[...]] * 8, axis=1)
    keep = jnp.where(row + 1 <= cuts, 2.0 / (n_ta * gr.shape[1]), 0.0)
    across.wait()

    total = []
    for h, c in ((0, new_a), (1, new_b)):
        parts = [pr[5 * h + i] for i in range(5)]
        tiles = list(parts)
        for first in (80, 96, 112):
            tile = left(parts[0], first)
            for i in range(1, 5):
                tile = jnp.where(lane < 16 * i, tile, left(parts[i], first - 16 * i))
            tiles.append(tile)
        total.append((c + sign * jnp.concatenate(tiles, axis=0)) * keep)
    both = jnp.concatenate(total, axis=0)
    mean_mode = (zero8 + pr[10])[0:1] * (1.0 / (n_ta * gr.shape[1]))
    filtered = jnp.dot(inverse[...], both, precision=highest, preferred_element_type=F32) + mean_mode
    bs[...] = filtered.reshape(bs.shape)

    b_copies = []
    for i in range(1, half):
        there = lax.rem(k + i, half)
        copy = remote(bs.at[there], br.at[k], b_send.at[i - 1], b_recv.at[i - 1], ta=base + there)
        copy.start()
        b_copies.append(copy)
    br[k] = bs[k]

    pl.when(has_low)(fx_up.wait_recv)
    pl.when(has_high)(fx_down.wait_recv)
    inv_rho0 = 1.0 / rho0

    def axial_part(x, carry):
        def axial(f):
            d = A1 * (fx[f, 4 + x] - fx[f, 2 + x]) + A2 * (fx[f, 5 + x] - fx[f, 1 + x])
            return d + A3 * (fx[f, 6 + x] - fx[f, x])

        along = DT * mean[pl.ds(x, 1)]
        d_u, d_p = axial(1), axial(4)
        out[0, x] = out[0, x] - along * axial(0) + damp_rho * d_u
        out[1, x] = out[1, x] - along * d_u + damp_v * d_p
        out[2, x] = out[2, x] - along * axial(2)
        out[3, x] = out[3, x] - along * axial(3)
        out[4, x] = out[4, x] - along * d_p - DT * d_u
        return carry

    lax.fori_loop(0, 8, axial_part, 0)

    for copy in b_copies:
        copy.wait()

    def merge(x, carry):
        t = br[x]
        for f in range(5):
            out[f, x] = jnp.where(lane < NF, left(t, 16 * f) if f else t, out[f, x])
        return carry

    lax.fori_loop(0, 8, merge, 0)

    pl.when(has_high)(lambda: each(h_up, "wait_send"))
    pl.when(has_low)(lambda: each(h_down, "wait_send"))
    pl.when(has_high)(fx_up.wait_send)
    pl.when(has_low)(fx_down.wait_send)
    th_down.wait_send()
    th_up.wait_send()


def tables(points, n_theta):
    n = np.arange(points)
    m = np.arange(1, MODES + 1)
    phase = (m[:, None] * n[None, :] % n_theta) * (2.0 * math.pi / n_theta)
    forward = np.concatenate([np.cos(phase), np.sin(phase)]).astype(np.float32)
    return forward, np.ascontiguousarray(forward.T)


def solution(mesh):
    n_gx, n_ta = mesh.shape["gx"], mesh.shape["ta"]

    def on_device(fields, mean_axial, cycle_mean_density, pml_layer, cycle_cutoff):
        nf, nx, nt, nr = fields.shape
        n_theta = nt * n_ta
        forward, inverse = tables(n_theta // 2, n_theta)
        vmem = pl.BlockSpec(memory_space=pltpu.VMEM)
        half = n_ta // 2
        dma = pltpu.SemaphoreType.DMA
        return pl.pallas_call(
            functools.partial(body, n_gx, n_ta, 2.0 * math.pi / n_theta),
            out_shape=pltpu.VMEM(fields.shape, F32),
            in_specs=[pl.BlockSpec(memory_space=pltpu.HBM)] * 7,
            out_specs=vmem,
            scratch_shapes=[
                pltpu.VMEM((nx, nr), F32),
                pltpu.VMEM((1, nr), F32),
                pltpu.VMEM((nx, nr), jnp.int32),
                pltpu.VMEM((1, NF), jnp.int32),
                pltpu.VMEM(forward.shape, F32),
                pltpu.VMEM(inverse.shape, F32),
                dma((6,)),
                pltpu.VMEM((nf, nx + 6, nt, nr), F32),
                pltpu.VMEM((2, nx, nt + 16, nr), F32),
                pltpu.VMEM((nx + 6, nt, nr), F32),
                pltpu.VMEM((nx, nt, nr), F32),
                pltpu.VMEM((nx, nt, nr), F32),
                pltpu.VMEM((nx, nt, nr), F32),
                pltpu.VMEM((nx, nt, nr), F32),
                pltpu.VMEM((nx, nt, nr), F32),
                pltpu.VMEM((6, nt, nr), F32),
                pltpu.VMEM((half, nt, nr), F32),
                pltpu.VMEM((2, nx, 8, nr), F32),
                pltpu.VMEM((2, nx, 8, nr), F32),
                pltpu.VMEM((11, 8, nr), F32),
                pltpu.VMEM((11, 8, nr), F32),
                pltpu.VMEM((nx, nt, nr), F32),
                pltpu.VMEM((nx, nt, nr), F32),
                pltpu.VMEM((nx, nr), F32),
                pltpu.VMEM((nx, nr), F32),
                pltpu.VMEM((nx, nr), F32),
                dma((2,)),
                dma((2,)), dma((2,)),
                dma((2,)), dma((2,)),
                dma((6,)), dma((half,)),
                dma((half - 1,)), dma((half - 1,)),
                dma, dma,
                dma((half - 1,)), dma((half - 1,)),
                pltpu.SemaphoreType.REGULAR,
            ],
            compiler_params=pltpu.CompilerParams(
                collective_id=0, has_side_effects=True, vmem_limit_bytes=40 * 1024 * 1024
            ),
        )(*[pltpu.with_memory_space_constraint(a, pltpu.HBM) for a in (
            fields,
            mean_axial,
            cycle_mean_density.reshape(1, nr),
            pml_layer,
            cycle_cutoff.reshape(1, NF),
            jnp.asarray(forward),
            jnp.asarray(inverse),
        )])

    return jax.shard_map(
        on_device,
        mesh=mesh,
        in_specs=(P(None, "gx", "ta", None), P("gx", None), P(), P("gx", None), P()),
        out_specs=P(None, "gx", "ta", None),
        check_vma=False,
    )
```

```python
import functools
import math

import jax
import jax.numpy as jnp
import numpy as np
from jax import lax
from jax.experimental import pallas as pl
from jax.experimental.pallas import tpu as pltpu
from jax.sharding import PartitionSpec as P

NF = 16
PMLW = 12
MODES = 64
LANES = 128
RUN = 8

A1, A2, A3 = 0.770882380518, -0.166705904415, 0.020843142770
DT = 0.1
PEAK = 4.0
F32 = jnp.float32
MESH = pl.DeviceIdType.MESH


def left(x, by):
    return pltpu.roll(x, LANES - by, x.ndim - 1)


def right(x, by):
    return pltpu.roll(x, by, x.ndim - 1)


def periodic(x, lane):
    x = jnp.where(lane < NF, x, 0.0)
    x = x + right(x, 16)
    x = x + right(x, 32)
    return x + right(x, 64)


def group(lane, g):
    return (lane >= NF * g) & (lane < NF * (g + 1))


def body(
    n_gx, n_ta, run, spacing,
    fields, *rest,
):
    inputs, rest = rest[:6], rest[6:]
    out, rest = rest[0], rest[1:]
    local, rest = rest[:6], rest[6:]
    input_sem, rest = rest[0], rest[1:]
    mean, dens, pml, cut, forward, inverse = local
    (
    fx, ext, rx, ex, zr, dp, qs, gr, hs, hr, th_out, th_in, ps, pr, bs, br, mt, st, sg,
    load_sem, ring_send, ring_recv, th_send, th_recv, h_send, h_recv,
    a_send, a_recv, z_send, z_recv, b_send, b_recv, far,
    ) = rest
    half = n_ta // 2
    gx = lax.axis_index("gx")
    ta = lax.axis_index("ta")
    k = lax.rem(ta, half)
    base = ta - k
    other = lax.rem(base + half, n_ta)
    partner = lax.rem(ta + half, n_ta)
    after = lax.rem(ta + 1, n_ta)
    before = lax.rem(ta + n_ta - 1, n_ta)
    has_low = gx > 0
    has_high = gx < n_gx - 1
    low = jnp.maximum(gx - 1, 0)
    high = jnp.minimum(gx + 1, n_gx - 1)
    edge_low = k == 0
    edge_high = k == half - 1
    farthest_first = sorted(range(1, half), key=lambda i: -min(i, half - i))
    second = ta >= half
    first = jnp.logical_not(second)
    cross_low = has_low & (lax.rem(gx, run) == 0)
    cross_high = has_high & (lax.rem(gx, run) == run - 1)
    ends = cross_low | cross_high
    mates = [base + lax.rem(k + i, half) for i in range(1, half)]
    takes_low = k < 3
    takes_high = k > half - 4

    loads = [pltpu.make_async_copy(fields.at[f], fx.at[f, 3:11], load_sem.at[f]) for f in range(5)]
    load_t = pltpu.make_async_copy(fields.at[3:5], ext.at[:, :, 8:40], load_sem.at[5])
    for copy in loads:
        copy.start()
    small = [pltpu.make_async_copy(inputs[i], local[i], input_sem.at[i]) for i in range(6)]
    for copy in small:
        copy.start()
    load_t.start()

    barrier = pltpu.get_barrier_semaphore()

    def greet(sem, **where):
        pl.semaphore_signal(sem, inc=1, device_id=where, device_id_type=MESH)

    def greet_across(sem):
        greet(sem, ta=partner)
        pl.when(edge_low)(lambda: greet(sem, ta=before))
        pl.when(edge_high)(lambda: greet(sem, ta=after))

    for mate in mates:
        greet(barrier, ta=mate)
    pl.when(first)(lambda: greet_across(barrier))
    for exists, takes, cross, there in (
        (has_low, takes_low, cross_low, low),
        (has_high, takes_high, cross_high, high),
    ):

        @pl.when(exists)
        def _():
            near_half = takes & (first | jnp.logical_not(cross))
            pl.when(jnp.logical_not(near_half))(lambda: greet(barrier, gx=there))

            @pl.when(near_half)
            def _():
                for j in range(half):
                    greet(barrier, gx=there, ta=base + j)

            @pl.when(takes & cross & first)
            def _():
                for j in range(half):
                    greet(barrier, gx=there, ta=other + j)

    for copy in small[:4]:
        copy.wait()

    lane = lax.broadcasted_iota(jnp.int32, (1, LANES), 1)
    lane8 = lax.broadcasted_iota(jnp.int32, (8, LANES), 1)
    inv_r = 1.0 / (lane.astype(F32) + 0.5)
    inv_dt = 1.0 / spacing
    rho0 = dens[...]
    depth = pml[...].astype(F32) / PMLW
    damp = 1.0 - DT * (PEAK * depth * depth)
    st[...] = damp
    mt[...] = periodic(mean[...], lane8)
    sg[...] = periodic(damp, lane8)
    rho0_p = periodic(jnp.broadcast_to(rho0, (8, LANES)), lane8)[0:1]
    inv_r_p = periodic(jnp.broadcast_to(inv_r, (8, LANES)), lane8)[0:1]

    def on(g, value):
        return jnp.where(group(lane, g), value, 0.0)

    up_w = [jnp.where(lane < LANES - s, a, 0.0) for s, a in ((1, A1), (2, A2), (3, A3))]
    dn_w = [jnp.where(lane >= s, a, 0.0) for s, a in ((1, A1), (2, A2), (3, A3))]
    g_0 = jnp.where(lane == 0, A1, jnp.where(lane == 1, A3, 0.0))
    g_u1 = jnp.where(lane == 0, A2, 0.0)
    g_u2 = jnp.where(lane == 0, A3, 0.0)
    g_d1 = jnp.where(lane == 1, A2, 0.0)
    g_d2 = jnp.where(lane == 2, A3, 0.0)
    c_e = on(0, -DT * rho0_p) + on(2, -DT / rho0_p) + on(4, -DT)

    def radial(f):
        ups = [left(f, s) for s in (1, 2, 3)]
        dns = [right(f, s) for s in (1, 2, 3)]
        d = (up_w[0] * ups[0] - dn_w[0] * dns[0]) + (up_w[1] * ups[1] - dn_w[1] * dns[1])
        d = d + (up_w[2] * ups[2] - dn_w[2] * dns[2])
        ghost = g_0 * f + g_u1 * ups[0] + g_u2 * ups[1] + g_d1 * dns[0] + g_d2 * dns[1]
        return d, ghost

    for copy in loads:
        copy.wait()

    def pack(x, carry):
        rho, u, v, w, p = (fx[f, 3 + x] for f in range(5))
        dv, gv = radial(v)
        dpr, gp = radial(p)
        z = dv + v * inv_r
        zr[x] = z
        dp[x] = dpr
        r = jnp.where(lane < 96, right(w, 80), jnp.where(lane < 112, right(p, 96), right(gv, 112) + right(gp, 115)))
        r = jnp.where(lane < 80, right(p, 64), r)
        r = jnp.where(lane < 64, right(w, 48), r)
        r = jnp.where(lane < 48, right(v, 32), r)
        r = jnp.where(lane < 32, right(u, 16), r)
        r = jnp.where(lane < 16, rho, r)
        rx[3 + x] = r
        e = jnp.where(lane < 16, z, jnp.where(lane < 48, right(dpr, 32), right(z, 64)))
        ex[x] = e * c_e
        return carry

    rx[0:3] = jnp.zeros((3,) + rx.shape[1:], F32)
    rx[11:14] = jnp.zeros((3,) + rx.shape[1:], F32)
    lax.fori_loop(0, 8, pack, 0, unroll=True)

    c_a = on(0, -DT * rho0_p)
    c_b = on(1, -DT / rho0_p)
    c_c = on(4, -DT)
    fields_only = lane < 5 * NF

    def advected(d, speed):
        return c_a * left(d, 16) + c_b * left(d, 48) + c_c * right(d, 48) - (DT * speed) * d

    def step_inner(x, carry):
        d = A1 * (rx[4 + x] - rx[2 + x]) + A2 * (rx[5 + x] - rx[1 + x]) + A3 * (rx[6 + x] - rx[x])
        r = rx[3 + x]
        row = pl.ds(x, 1)
        s = r * sg[row] + advected(d, mt[row]) + ex[x]
        qs[x] = jnp.where(fields_only, s, r)
        return carry

    lax.fori_loop(0, 8, step_inner, 0, unroll=True)
    hs[0] = -(A1 * rx[10] + A2 * rx[9] + A3 * rx[8])
    hs[1] = -(A2 * rx[10] + A3 * rx[9])
    hs[2] = -A3 * rx[10]
    hs[3] = A3 * rx[3]
    hs[4] = A2 * rx[3] + A3 * rx[4]
    hs[5] = A1 * rx[3] + A2 * rx[4] + A3 * rx[5]

    comes = (takes_low & has_low & (first | jnp.logical_not(cross_low))) | (
        takes_high & has_high & (first | jnp.logical_not(cross_high))
    )
    comes_across = first & ((takes_low & cross_low) | (takes_high & cross_high))

    @pl.when(jnp.logical_not(comes))
    def _():
        hr[0] = jnp.zeros(hr.shape[1:], F32)

    @pl.when(jnp.logical_not(comes_across))
    def _():
        hr[1] = jnp.zeros(hr.shape[1:], F32)

    def count(flag):
        return flag.astype(jnp.int32)

    crossing = 1 + count(edge_low) + count(edge_high)
    from_low = count(has_low) * (4 - count(takes_high & (first | jnp.logical_not(cross_low))))
    from_high = count(has_high) * (4 - count(takes_low & (first | jnp.logical_not(cross_high))))
    pl.semaphore_wait(barrier, half - 1 + from_low + from_high + count(second) * crossing)
    pl.when(second)(lambda: greet_across(far))

    def remote(src, dst, send, recv, **where):
        return pltpu.make_async_remote_copy(
            src_ref=src, dst_ref=dst, send_sem=send, recv_sem=recv, device_id=where, device_id_type=MESH
        )

    def halo(j, there, target, way):
        return remote(hs.at[j], hr.at[way, k], h_send.at[j], h_recv.at[way, k], gx=there, ta=target)

    h_up = [halo(j, high, base + j, 0) for j in range(3)]
    h_up_across = [halo(j, high, other + j, 1) for j in range(3)]
    h_down = [halo(j, low, base + half - 6 + j, 0) for j in range(3, 6)]
    h_down_across = [halo(j, low, other + half - 6 + j, 1) for j in range(3, 6)]
    fx_up = remote(fx.at[:, 8:11], fx.at[:, 0:3], ring_send.at[0], ring_recv.at[0], gx=high)
    fx_down = remote(fx.at[:, 3:6], fx.at[:, 11:14], ring_send.at[1], ring_recv.at[1], gx=low)
    th_down = remote(th_out.at[0], th_in.at[1], th_send.at[0], th_recv.at[1], ta=before)
    th_up = remote(th_out.at[1], th_in.at[0], th_send.at[1], th_recv.at[0], ta=after)

    def each(copies, method):
        for copy in copies:
            getattr(copy, method)()

    a_copies = []
    for i in farthest_first:
        there = lax.rem(k + i, half)
        copy = remote(qs.at[there], gr.at[k], a_send.at[i - 1], a_recv.at[i - 1], ta=base + there)
        copy.start()
        a_copies.append(copy)
    pl.when(has_high & (first | jnp.logical_not(cross_high)))(lambda: each(h_up, "start"))
    pl.when(has_low & (first | jnp.logical_not(cross_low)))(lambda: each(h_down, "start"))
    pl.when(cross_high & second)(lambda: each(h_up_across, "start"))
    pl.when(cross_low & second)(lambda: each(h_down_across, "start"))
    gr[k] = qs[k]

    def pack_edges(x, carry):
        for f in range(2):
            th_out[0, x, 3 * f : 3 * f + 3] = ext[f, x, 8:11]
            th_out[1, x, 3 * f : 3 * f + 3] = ext[f, x, 37:40]
        return carry

    load_t.wait()
    th_out[...] = jnp.zeros_like(th_out)
    lax.fori_loop(0, 8, pack_edges, 0)
    pl.when(second | jnp.logical_not(edge_low))(th_down.start)
    pl.when(second | jnp.logical_not(edge_high))(th_up.start)

    near_low = has_low & jnp.logical_not(cross_low)
    near_high = has_high & jnp.logical_not(cross_high)
    near_low = has_low & jnp.logical_not(cross_low)
    near_high = has_high & jnp.logical_not(cross_high)
    middle = jnp.logical_not(ends)
    pl.when(cross_high & first)(fx_up.start)
    pl.when(near_high & cross_low & first)(fx_up.start)
    pl.when(near_high & first & middle)(fx_up.start)
    pl.when(near_low & first & middle)(fx_down.start)

    @pl.when(jnp.logical_not(has_low))
    def _():
        fx[:, 0:3] = jnp.zeros((5, 3) + fx.shape[2:], F32)

    @pl.when(jnp.logical_not(has_high))
    def _():
        fx[:, 11:14] = jnp.zeros((5, 3) + fx.shape[2:], F32)

    @pl.when(first)
    def _():
        pl.semaphore_wait(far, crossing)
        pl.when(edge_low)(th_down.start)
        pl.when(edge_high)(th_up.start)

    each(a_copies, "wait_recv")
    for copy in small[4:]:
        copy.wait()

    for way, flag in ((0, comes), (1, comes_across)):

        @pl.when(flag)
        def _():
            for j in range(half):
                remote(hs.at[0], hr.at[way, j], h_send.at[0], h_recv.at[way, j], gx=low).wait_recv()

    speed = jnp.where(fields_only, mt[pl.ds(k, 1)], 0.0)
    rows = half * gr.shape[1]
    parts = [gr[...], hr[0], hr[1]]
    g = jnp.concatenate([part.reshape(rows, LANES) for part in parts], axis=1)
    highest = lax.Precision.HIGHEST
    coef = jnp.dot(forward[...], g, precision=highest, preferred_element_type=F32)
    kappa = 2.0 * (A1 * forward[MODES:, 1:2] + A2 * forward[MODES:, 2:3] + A3 * forward[MODES:, 3:4])
    row = lax.broadcasted_iota(jnp.int32, (MODES, LANES), 0)
    sign = jnp.where(lax.rem(row, 2) == 1, 1.0, -1.0)
    zero_mode = jnp.sum(g, axis=0, keepdims=True)
    zero_mode = zero_mode[:, :LANES] + advected(zero_mode[:, LANES : 2 * LANES] + zero_mode[:, 2 * LANES :], speed)

    def gathered(c):
        return c[:, :LANES] + advected(c[:, LANES : 2 * LANES] + sign * c[:, 2 * LANES :], speed)

    a_m, b_m = gathered(coef[:MODES]), gathered(coef[MODES:])
    around_p = -DT * inv_r_p * inv_dt
    t_r, t_p, t_w = on(0, around_p * rho0_p), on(4, around_p), on(3, around_p / rho0_p)
    three = lane < 3
    h_r = jnp.where(three, -DT * rho0_p, 0.0)
    h_p = jnp.where((lane >= 64) & (lane < 67), -DT, 0.0)
    h_v = jnp.where((lane >= 32) & (lane < 35), DT / rho0_p, 0.0)

    def turned(c):
        return t_r * left(c, 80) + t_p * left(c, 16) + t_w * left(c, 48)

    def mirrored(c):
        return h_r * left(c, 112) + h_p * left(c, 48) + h_v * left(c, 83)

    new_a = a_m + turned(kappa * b_m) + sign * mirrored(a_m)
    new_b = b_m - turned(kappa * a_m) + sign * mirrored(b_m)
    zero8 = jnp.broadcast_to(zero_mode, (8, LANES))
    zero8 = zero8 + mirrored(zero8)

    for h, c in ((0, new_a), (1, new_b)):
        t5, t6, t7 = c[40:48], c[48:56], c[56:64]
        for i in range(5):
            spread = jnp.where(lane < 112, right(t6, 96 - 16 * i), right(t7, 112 - 16 * i))
            spread = jnp.where(lane < 96, right(t5, 80 - 16 * i), spread)
            ps[5 * h + i] = jnp.where(lane < 80, c[8 * i : 8 * i + 8], spread)
    ps[10] = zero8
    across = remote(ps, pr, z_send, z_recv, ta=partner)

    across.start()
    pl.when(cross_low & first)(fx_down.start)
    pl.when(near_low & cross_high & first)(fx_down.start)
    damp_rho = -DT * rho0
    damp_v = -DT / rho0

    def local_part(x, carry):
        keep = st[pl.ds(x, 1)]
        z = zr[x]
        out[0, x] = fx[0, 3 + x] * keep + damp_rho * z
        out[1, x] = fx[1, 3 + x] * keep
        out[2, x] = fx[2, 3 + x] * keep + damp_v * dp[x]
        out[3, x] = fx[3, 3 + x] * keep
        out[4, x] = fx[4, 3 + x] * keep - DT * z
        return carry

    lax.fori_loop(0, 8, local_part, 0)
    pl.when(cross_low & second)(fx_down.start)
    pl.when(cross_high & second)(fx_up.start)
    pl.when(near_high & second & middle)(fx_up.start)
    pl.when(near_low & second & middle)(fx_down.start)
    pl.when(near_high & cross_low & second)(fx_up.start)
    pl.when(near_low & cross_high & second)(fx_down.start)
    th_up.wait_recv()
    th_down.wait_recv()
    around = inv_r * inv_dt

    def angular_part(x, carry):
        for f in range(2):
            ext[f, x, 5:8] = th_in[0, x, 3 * f : 3 * f + 3]
            ext[f, x, 40:43] = th_in[1, x, 3 * f : 3 * f + 3]

        def angular(f):
            d = A1 * (ext[f, x, 9:41] - ext[f, x, 7:39]) + A2 * (ext[f, x, 10:42] - ext[f, x, 6:38])
            return (d + A3 * (ext[f, x, 11:43] - ext[f, x, 5:37])) * around

        d_w = angular(0)
        out[0, x] = out[0, x] + damp_rho * d_w
        out[3, x] = out[3, x] + damp_v * angular(1)
        out[4, x] = out[4, x] - DT * d_w
        return carry

    lax.fori_loop(0, 8, angular_part, 0)

    cuts = jnp.concatenate([cut[...]] * 8, axis=1)
    keep = jnp.where(row + 1 <= cuts, 2.0 / (n_ta * gr.shape[1]), 0.0)
    across.wait_recv()

    total = []
    for h, c in ((0, new_a), (1, new_b)):
        parts = [pr[5 * h + i] for i in range(5)]
        tiles = list(parts)
        for first in (80, 96, 112):
            tile = left(parts[0], first)
            for i in range(1, 5):
                tile = jnp.where(lane < 16 * i, tile, left(parts[i], first - 16 * i))
            tiles.append(tile)
        total.append((c + sign * jnp.concatenate(tiles, axis=0)) * keep)
    both = jnp.concatenate(total, axis=0)
    mean_mode = (zero8 + pr[10])[0:1] * (1.0 / (n_ta * gr.shape[1]))
    filtered = jnp.dot(inverse[...], both, precision=highest, preferred_element_type=F32) + mean_mode
    bs[...] = filtered.reshape(bs.shape)

    b_copies = []
    for i in farthest_first:
        there = lax.rem(k + i, half)
        copy = remote(bs.at[there], br.at[k], b_send.at[i - 1], b_recv.at[i - 1], ta=base + there)
        copy.start()
        b_copies.append(copy)
    br[k] = bs[k]

    pl.when(has_low)(fx_up.wait_recv)
    pl.when(has_high)(fx_down.wait_recv)
    inv_rho0 = 1.0 / rho0

    def axial_part(x, carry):
        def axial(f):
            d = A1 * (fx[f, 4 + x] - fx[f, 2 + x]) + A2 * (fx[f, 5 + x] - fx[f, 1 + x])
            return d + A3 * (fx[f, 6 + x] - fx[f, x])

        along = DT * mean[pl.ds(x, 1)]
        d_u, d_p = axial(1), axial(4)
        out[0, x] = out[0, x] - along * axial(0) + damp_rho * d_u
        out[1, x] = out[1, x] - along * d_u + damp_v * d_p
        out[2, x] = out[2, x] - along * axial(2)
        out[3, x] = out[3, x] - along * axial(3)
        out[4, x] = out[4, x] - along * d_p - DT * d_u
        return carry

    lax.fori_loop(0, 8, axial_part, 0)

    each(b_copies, "wait_recv")

    def merge(x, carry):
        t = br[x]
        for f in range(5):
            out[f, x] = jnp.where(lane < NF, left(t, 16 * f) if f else t, out[f, x])
        return carry

    lax.fori_loop(0, 8, merge, 0)

    pl.when(has_high)(lambda: each(h_up, "wait_send"))
    pl.when(has_low)(lambda: each(h_down, "wait_send"))
    pl.when(has_high)(fx_up.wait_send)
    pl.when(has_low)(fx_down.wait_send)
    each(a_copies + [across] + b_copies + [th_down, th_up], "wait_send")


def tables(points, n_theta):
    n = np.arange(points)
    m = np.arange(1, MODES + 1)
    phase = (m[:, None] * n[None, :] % n_theta) * (2.0 * math.pi / n_theta)
    forward = np.concatenate([np.cos(phase), np.sin(phase)]).astype(np.float32)
    return forward, np.ascontiguousarray(forward.T)


def solution(mesh):
    n_gx, n_ta = mesh.shape["gx"], mesh.shape["ta"]

    def on_device(fields, mean_axial, cycle_mean_density, pml_layer, cycle_cutoff):
        nf, nx, nt, nr = fields.shape
        n_theta = nt * n_ta
        forward, inverse = tables(n_theta // 2, n_theta)
        vmem = pl.BlockSpec(memory_space=pltpu.VMEM)
        half = n_ta // 2
        dma = pltpu.SemaphoreType.DMA
        return pl.pallas_call(
            functools.partial(body, n_gx, n_ta, RUN, 2.0 * math.pi / n_theta),
            out_shape=pltpu.VMEM(fields.shape, F32),
            in_specs=[pl.BlockSpec(memory_space=pltpu.HBM)] * 7,
            out_specs=vmem,
            scratch_shapes=[
                pltpu.VMEM((nx, nr), F32),
                pltpu.VMEM((1, nr), F32),
                pltpu.VMEM((nx, nr), jnp.int32),
                pltpu.VMEM((1, NF), jnp.int32),
                pltpu.VMEM(forward.shape, F32),
                pltpu.VMEM(inverse.shape, F32),
                dma((6,)),
                pltpu.VMEM((nf, nx + 6, nt, nr), F32),
                pltpu.VMEM((2, nx, nt + 16, nr), F32),
                pltpu.VMEM((nx + 6, nt, nr), F32),
                pltpu.VMEM((nx, nt, nr), F32),
                pltpu.VMEM((nx, nt, nr), F32),
                pltpu.VMEM((nx, nt, nr), F32),
                pltpu.VMEM((nx, nt, nr), F32),
                pltpu.VMEM((nx, nt, nr), F32),
                pltpu.VMEM((6, nt, nr), F32),
                pltpu.VMEM((2, half, nt, nr), F32),
                pltpu.VMEM((2, nx, 8, nr), F32),
                pltpu.VMEM((2, nx, 8, nr), F32),
                pltpu.VMEM((11, 8, nr), F32),
                pltpu.VMEM((11, 8, nr), F32),
                pltpu.VMEM((nx, nt, nr), F32),
                pltpu.VMEM((nx, nt, nr), F32),
                pltpu.VMEM((nx, nr), F32),
                pltpu.VMEM((nx, nr), F32),
                pltpu.VMEM((nx, nr), F32),
                dma((6,)),
                dma((2,)), dma((2,)),
                dma((2,)), dma((2,)),
                dma((6,)), dma((2, half)),
                dma((half - 1,)), dma((half - 1,)),
                dma, dma,
                dma((half - 1,)), dma((half - 1,)),
                pltpu.SemaphoreType.REGULAR,
            ],
            compiler_params=pltpu.CompilerParams(
                collective_id=0, has_side_effects=True, vmem_limit_bytes=40 * 1024 * 1024
            ),
        )(*[pltpu.with_memory_space_constraint(a, pltpu.HBM) for a in (
            fields,
            mean_axial,
            cycle_mean_density.reshape(1, nr),
            pml_layer,
            cycle_cutoff.reshape(1, NF),
            jnp.asarray(forward),
            jnp.asarray(inverse),
        )])

    return jax.shard_map(
        on_device,
        mesh=mesh,
        in_specs=(P(None, "gx", "ta", None), P("gx", None), P(), P("gx", None), P()),
        out_specs=P(None, "gx", "ta", None),
        check_vma=False,
    )
```

```python
import functools
import math

import jax
import jax.numpy as jnp
import numpy as np
from jax import lax
from jax.experimental import pallas as pl
from jax.experimental.pallas import tpu as pltpu
from jax.sharding import PartitionSpec as P

NF = 16
PMLW = 12
MODES = 64
LANES = 128
RUN = 8

A1, A2, A3 = 0.770882380518, -0.166705904415, 0.020843142770
DT = 0.1
PEAK = 4.0
F32 = jnp.float32
MESH = pl.DeviceIdType.MESH


def left(x, by):
    return pltpu.roll(x, LANES - by, x.ndim - 1)


def right(x, by):
    return pltpu.roll(x, by, x.ndim - 1)


def periodic(x, lane):
    x = jnp.where(lane < NF, x, 0.0)
    x = x + right(x, 16)
    x = x + right(x, 32)
    return x + right(x, 64)


def group(lane, g):
    return (lane >= NF * g) & (lane < NF * (g + 1))


def narrow(x, lane):
    last = x[..., 24:32, :]
    first = jnp.where(lane < 80, x[..., 0:8, :], right(last, 80))
    second = jnp.where(lane < 80, x[..., 8:16, :], right(last, 32))
    return jnp.concatenate([first, second, x[..., 16:24, :]], axis=-2)


def widen(x, lane):
    last = jnp.where(lane < 48, left(x[..., 0:8, :], 80), left(x[..., 8:16, :], 32))
    return jnp.concatenate([x, last], axis=-2)


def body(
    n_gx, n_ta, run, spacing,
    fields, *rest,
):
    inputs, rest = rest[:6], rest[6:]
    out, rest = rest[0], rest[1:]
    local, rest = rest[:6], rest[6:]
    input_sem, rest = rest[0], rest[1:]
    mean, dens, pml, cut, forward, inverse = local
    (
    fx, ext, rx, ex, zr, dp, qs, gr, hs, hr, th_out, th_in, ps, pr, bs, br, mt, st, sg,
    load_sem, ring_send, ring_recv, th_send, th_recv, h_send, h_recv,
    a_send, a_recv, z_send, z_recv, b_send, b_recv, far,
    ) = rest
    half = n_ta // 2
    gx = lax.axis_index("gx")
    ta = lax.axis_index("ta")
    k = lax.rem(ta, half)
    base = ta - k
    other = lax.rem(base + half, n_ta)
    partner = lax.rem(ta + half, n_ta)
    after = lax.rem(ta + 1, n_ta)
    before = lax.rem(ta + n_ta - 1, n_ta)
    has_low = gx > 0
    has_high = gx < n_gx - 1
    low = jnp.maximum(gx - 1, 0)
    high = jnp.minimum(gx + 1, n_gx - 1)
    edge_low = k == 0
    edge_high = k == half - 1
    farthest_first = sorted(range(1, half), key=lambda i: -min(i, half - i))
    second = ta >= half
    first = jnp.logical_not(second)
    cross_low = has_low & (lax.rem(gx, run) == 0)
    cross_high = has_high & (lax.rem(gx, run) == run - 1)
    ends = cross_low | cross_high
    mates = [base + lax.rem(k + i, half) for i in range(1, half)]
    takes_low = k < 3
    takes_high = k > half - 4

    loads = [pltpu.make_async_copy(fields.at[f], fx.at[f, 3:11], load_sem.at[f]) for f in range(5)]
    load_t = pltpu.make_async_copy(fields.at[3:5], ext.at[:, :, 8:40], load_sem.at[5])
    for copy in loads:
        copy.start()
    small = [pltpu.make_async_copy(inputs[i], local[i], input_sem.at[i]) for i in range(6)]
    for copy in small:
        copy.start()
    load_t.start()

    barrier = pltpu.get_barrier_semaphore()

    def greet(sem, **where):
        pl.semaphore_signal(sem, inc=1, device_id=where, device_id_type=MESH)

    def greet_across(sem):
        greet(sem, ta=partner)
        pl.when(edge_low)(lambda: greet(sem, ta=before))
        pl.when(edge_high)(lambda: greet(sem, ta=after))

    for mate in mates:
        greet(barrier, ta=mate)
    pl.when(first)(lambda: greet_across(barrier))
    for exists, takes, cross, there in (
        (has_low, takes_low, cross_low, low),
        (has_high, takes_high, cross_high, high),
    ):

        @pl.when(exists)
        def _():
            near_half = takes & (first | jnp.logical_not(cross))
            pl.when(jnp.logical_not(near_half))(lambda: greet(barrier, gx=there))

            @pl.when(near_half)
            def _():
                for j in range(half):
                    greet(barrier, gx=there, ta=base + j)

            @pl.when(takes & cross & first)
            def _():
                for j in range(half):
                    greet(barrier, gx=there, ta=other + j)

    for copy in small[:4]:
        copy.wait()

    lane = lax.broadcasted_iota(jnp.int32, (1, LANES), 1)
    lane8 = lax.broadcasted_iota(jnp.int32, (8, LANES), 1)
    inv_r = 1.0 / (lane.astype(F32) + 0.5)
    inv_dt = 1.0 / spacing
    rho0 = dens[...]
    depth = pml[...].astype(F32) / PMLW
    damp = 1.0 - DT * (PEAK * depth * depth)
    st[...] = damp
    mt[...] = periodic(mean[...], lane8)
    sg[...] = periodic(damp, lane8)
    rho0_p = periodic(jnp.broadcast_to(rho0, (8, LANES)), lane8)[0:1]
    inv_r_p = periodic(jnp.broadcast_to(inv_r, (8, LANES)), lane8)[0:1]

    def on(g, value):
        return jnp.where(group(lane, g), value, 0.0)

    up_w = [jnp.where(lane < LANES - s, a, 0.0) for s, a in ((1, A1), (2, A2), (3, A3))]
    dn_w = [jnp.where(lane >= s, a, 0.0) for s, a in ((1, A1), (2, A2), (3, A3))]
    g_0 = jnp.where(lane == 0, A1, jnp.where(lane == 1, A3, 0.0))
    g_u1 = jnp.where(lane == 0, A2, 0.0)
    g_u2 = jnp.where(lane == 0, A3, 0.0)
    g_d1 = jnp.where(lane == 1, A2, 0.0)
    g_d2 = jnp.where(lane == 2, A3, 0.0)
    c_e = on(0, -DT * rho0_p) + on(2, -DT / rho0_p) + on(4, -DT)

    def radial(f):
        ups = [left(f, s) for s in (1, 2, 3)]
        dns = [right(f, s) for s in (1, 2, 3)]
        d = (up_w[0] * ups[0] - dn_w[0] * dns[0]) + (up_w[1] * ups[1] - dn_w[1] * dns[1])
        d = d + (up_w[2] * ups[2] - dn_w[2] * dns[2])
        ghost = g_0 * f + g_u1 * ups[0] + g_u2 * ups[1] + g_d1 * dns[0] + g_d2 * dns[1]
        return d, ghost

    for copy in loads:
        copy.wait()

    def pack(x, carry):
        rho, u, v, w, p = (fx[f, 3 + x] for f in range(5))
        dv, gv = radial(v)
        dpr, gp = radial(p)
        z = dv + v * inv_r
        zr[x] = z
        dp[x] = dpr
        r = jnp.where(lane < 96, right(w, 80), jnp.where(lane < 112, right(p, 96), right(gv, 112) + right(gp, 115)))
        r = jnp.where(lane < 80, right(p, 64), r)
        r = jnp.where(lane < 64, right(w, 48), r)
        r = jnp.where(lane < 48, right(v, 32), r)
        r = jnp.where(lane < 32, right(u, 16), r)
        r = jnp.where(lane < 16, rho, r)
        rx[3 + x] = r
        e = jnp.where(lane < 16, z, jnp.where(lane < 48, right(dpr, 32), right(z, 64)))
        ex[x] = e * c_e
        return carry

    rx[0:3] = jnp.zeros((3,) + rx.shape[1:], F32)
    rx[11:14] = jnp.zeros((3,) + rx.shape[1:], F32)
    lax.fori_loop(0, 8, pack, 0, unroll=True)

    c_a = on(0, -DT * rho0_p)
    c_b = on(1, -DT / rho0_p)
    c_c = on(4, -DT)
    fields_only = lane < 5 * NF

    def advected(d, speed):
        return c_a * left(d, 16) + c_b * left(d, 48) + c_c * right(d, 48) - (DT * speed) * d

    def step_inner(x, carry):
        d = A1 * (rx[4 + x] - rx[2 + x]) + A2 * (rx[5 + x] - rx[1 + x]) + A3 * (rx[6 + x] - rx[x])
        r = rx[3 + x]
        row = pl.ds(x, 1)
        s = r * sg[row] + advected(d, mt[row]) + ex[x]
        qs[x] = jnp.where(fields_only, s, r)
        return carry

    lax.fori_loop(0, 8, step_inner, 0, unroll=True)
    edge = [rx[x] for x in (3, 4, 5, 8, 9, 10)]
    for j, combined in enumerate(
        (
            -(A1 * edge[5] + A2 * edge[4] + A3 * edge[3]),
            -(A2 * edge[5] + A3 * edge[4]),
            -A3 * edge[5],
            A3 * edge[0],
            A2 * edge[0] + A3 * edge[1],
            A1 * edge[0] + A2 * edge[1] + A3 * edge[2],
        )
    ):
        hs[j] = narrow(combined, lane)

    comes = (takes_low & has_low & (first | jnp.logical_not(cross_low))) | (
        takes_high & has_high & (first | jnp.logical_not(cross_high))
    )
    comes_across = first & ((takes_low & cross_low) | (takes_high & cross_high))

    @pl.when(jnp.logical_not(comes))
    def _():
        hr[0] = jnp.zeros(hr.shape[1:], F32)

    @pl.when(jnp.logical_not(comes_across))
    def _():
        hr[1] = jnp.zeros(hr.shape[1:], F32)

    def count(flag):
        return flag.astype(jnp.int32)

    crossing = 1 + count(edge_low) + count(edge_high)
    from_low = count(has_low) * (4 - count(takes_high & (first | jnp.logical_not(cross_low))))
    from_high = count(has_high) * (4 - count(takes_low & (first | jnp.logical_not(cross_high))))
    pl.semaphore_wait(barrier, half - 1 + from_low + from_high + count(second) * crossing)
    pl.when(second)(lambda: greet_across(far))

    def remote(src, dst, send, recv, **where):
        return pltpu.make_async_remote_copy(
            src_ref=src, dst_ref=dst, send_sem=send, recv_sem=recv, device_id=where, device_id_type=MESH
        )

    def halo(j, there, target, way):
        return remote(hs.at[j], hr.at[way, k], h_send.at[j], h_recv.at[way, k], gx=there, ta=target)

    h_up = [halo(j, high, base + j, 0) for j in range(3)]
    h_up_across = [halo(j, high, other + j, 1) for j in range(3)]
    h_down = [halo(j, low, base + half - 6 + j, 0) for j in range(3, 6)]
    h_down_across = [halo(j, low, other + half - 6 + j, 1) for j in range(3, 6)]
    def bulk(part, fs, way, src, dst, there):
        return remote(
            fx.at[fs, src : src + 3], fx.at[fs, dst : dst + 3], ring_send.at[way, part], ring_recv.at[way, part], gx=there
        )

    parts = ((0, pl.ds(0, 2)), (1, pl.ds(2, 3)))
    fx_up = [bulk(part, fs, 0, 8, 0, high) for part, fs in parts]
    fx_down = [bulk(part, fs, 1, 3, 11, low) for part, fs in parts]
    th_down = remote(th_out.at[0], th_in.at[1], th_send.at[0], th_recv.at[1], ta=before)
    th_up = remote(th_out.at[1], th_in.at[0], th_send.at[1], th_recv.at[0], ta=after)

    def each(copies, method):
        for copy in copies:
            getattr(copy, method)()

    a_copies = []
    for i in farthest_first:
        there = lax.rem(k + i, half)
        copy = remote(qs.at[there], gr.at[k], a_send.at[i - 1], a_recv.at[i - 1], ta=base + there)
        copy.start()
        a_copies.append(copy)
    pl.when(has_high & (first | jnp.logical_not(cross_high)))(lambda: each(h_up, "start"))
    pl.when(has_low & (first | jnp.logical_not(cross_low)))(lambda: each(h_down, "start"))
    pl.when(cross_high & second)(lambda: each(h_up_across, "start"))
    pl.when(cross_low & second)(lambda: each(h_down_across, "start"))
    gr[k] = qs[k]

    def pack_edges(x, carry):
        for f in range(2):
            th_out[0, x, 3 * f : 3 * f + 3] = ext[f, x, 8:11]
            th_out[1, x, 3 * f : 3 * f + 3] = ext[f, x, 37:40]
        return carry

    load_t.wait()
    th_out[...] = jnp.zeros_like(th_out)
    lax.fori_loop(0, 8, pack_edges, 0)
    pl.when(second | jnp.logical_not(edge_low))(th_down.start)
    pl.when(second | jnp.logical_not(edge_high))(th_up.start)

    near_low = has_low & jnp.logical_not(cross_low)
    near_high = has_high & jnp.logical_not(cross_high)
    near_low = has_low & jnp.logical_not(cross_low)
    near_high = has_high & jnp.logical_not(cross_high)
    middle = jnp.logical_not(ends)
    pl.when(cross_high & first)(lambda: each(fx_up, "start"))
    pl.when(near_high & cross_low & first)(lambda: each(fx_up, "start"))
    pl.when(near_high & first & middle)(lambda: each(fx_up, "start"))
    pl.when(near_low & first & middle)(lambda: each(fx_down, "start"))

    @pl.when(jnp.logical_not(has_low))
    def _():
        fx[:, 0:3] = jnp.zeros((5, 3) + fx.shape[2:], F32)

    @pl.when(jnp.logical_not(has_high))
    def _():
        fx[:, 11:14] = jnp.zeros((5, 3) + fx.shape[2:], F32)

    for copy in small[4:]:
        copy.wait()
    speed = jnp.where(fields_only, mt[pl.ds(k, 1)], 0.0)
    kappa = 2.0 * (A1 * forward[MODES:, 1:2] + A2 * forward[MODES:, 2:3] + A3 * forward[MODES:, 3:4])
    row = lax.broadcasted_iota(jnp.int32, (MODES, LANES), 0)
    sign = jnp.where(lax.rem(row, 2) == 1, 1.0, -1.0)
    around_p = -DT * inv_r_p * inv_dt
    t_r, t_p, t_w = on(0, around_p * rho0_p), on(4, around_p), on(3, around_p / rho0_p)
    three = lane < 3
    h_r = jnp.where(three, -DT * rho0_p, 0.0)
    h_p = jnp.where((lane >= 64) & (lane < 67), -DT, 0.0)
    h_v = jnp.where((lane >= 32) & (lane < 35), DT / rho0_p, 0.0)


    @pl.when(first)
    def _():
        pl.semaphore_wait(far, crossing)
        pl.when(edge_low)(th_down.start)
        pl.when(edge_high)(th_up.start)

    each(a_copies, "wait_recv")

    for way, flag in ((0, comes), (1, comes_across)):

        @pl.when(flag)
        def _():
            for j in range(half):
                remote(hs.at[0], hr.at[way, j], h_send.at[0], h_recv.at[way, j], gx=low).wait_recv()

    rows = half * gr.shape[1]
    sources = [gr[...], widen(hr[0], lane), widen(hr[1], lane)]
    g = jnp.concatenate([part.reshape(rows, LANES) for part in sources], axis=1)
    highest = lax.Precision.HIGHEST
    coef = jnp.dot(forward[...], g, precision=highest, preferred_element_type=F32)
    zero_mode = jnp.sum(g, axis=0, keepdims=True)
    zero_mode = zero_mode[:, :LANES] + advected(zero_mode[:, LANES : 2 * LANES] + zero_mode[:, 2 * LANES :], speed)

    def gathered(c):
        return c[:, :LANES] + advected(c[:, LANES : 2 * LANES] + sign * c[:, 2 * LANES :], speed)

    a_m, b_m = gathered(coef[:MODES]), gathered(coef[MODES:])
    def turned(c):
        return t_r * left(c, 80) + t_p * left(c, 16) + t_w * left(c, 48)

    def mirrored(c):
        return h_r * left(c, 112) + h_p * left(c, 48) + h_v * left(c, 83)

    new_a = a_m + turned(kappa * b_m) + sign * mirrored(a_m)
    new_b = b_m - turned(kappa * a_m) + sign * mirrored(b_m)
    zero8 = jnp.broadcast_to(zero_mode, (8, LANES))
    zero8 = zero8 + mirrored(zero8)

    for h, c in ((0, new_a), (1, new_b)):
        t5, t6, t7 = c[40:48], c[48:56], c[56:64]
        for i in range(5):
            spread = jnp.where(lane < 112, right(t6, 96 - 16 * i), right(t7, 112 - 16 * i))
            spread = jnp.where(lane < 96, right(t5, 80 - 16 * i), spread)
            ps[5 * h + i] = jnp.where(lane < 80, c[8 * i : 8 * i + 8], spread)
    ps[10] = zero8
    across = remote(ps, pr, z_send, z_recv, ta=partner)

    across.start()
    pl.when(cross_low & first)(lambda: each(fx_down, "start"))
    pl.when(near_low & cross_high & first)(lambda: each(fx_down, "start"))
    pl.when(near_high & second & middle)(lambda: each(fx_up, "start"))
    pl.when(near_low & second & middle)(lambda: each(fx_down, "start"))
    pl.when(near_high & cross_low & second)(fx_up[0].start)
    damp_rho = -DT * rho0
    damp_v = -DT / rho0

    def local_part(x, carry):
        keep = st[pl.ds(x, 1)]
        z = zr[x]
        out[0, x] = fx[0, 3 + x] * keep + damp_rho * z
        out[1, x] = fx[1, 3 + x] * keep
        out[2, x] = fx[2, 3 + x] * keep + damp_v * dp[x]
        out[3, x] = fx[3, 3 + x] * keep
        out[4, x] = fx[4, 3 + x] * keep - DT * z
        return carry

    lax.fori_loop(0, 8, local_part, 0)
    pl.when(cross_low & second)(lambda: each(fx_down, "start"))
    pl.when(near_high & cross_low & second)(fx_up[1].start)
    pl.when(cross_high & second)(lambda: each(fx_up, "start"))
    pl.when(near_low & cross_high & second)(lambda: each(fx_down, "start"))
    th_up.wait_recv()
    th_down.wait_recv()
    around = inv_r * inv_dt

    def angular_part(x, carry):
        for f in range(2):
            ext[f, x, 5:8] = th_in[0, x, 3 * f : 3 * f + 3]
            ext[f, x, 40:43] = th_in[1, x, 3 * f : 3 * f + 3]

        def angular(f):
            d = A1 * (ext[f, x, 9:41] - ext[f, x, 7:39]) + A2 * (ext[f, x, 10:42] - ext[f, x, 6:38])
            return (d + A3 * (ext[f, x, 11:43] - ext[f, x, 5:37])) * around

        d_w = angular(0)
        out[0, x] = out[0, x] + damp_rho * d_w
        out[3, x] = out[3, x] + damp_v * angular(1)
        out[4, x] = out[4, x] - DT * d_w
        return carry

    lax.fori_loop(0, 8, angular_part, 0)
    taps = ((1, A1), (2, A2), (3, A3))

    def add_axial(x, terms):
        def axial(f):
            total = None
            for weight, value in terms(f, x):
                total = weight * value if total is None else total + weight * value
            return total

        along = DT * mean[x : x + 1]
        d_u, d_p = axial(1), axial(4)
        out[0, x] = out[0, x] - along * axial(0) + damp_rho * d_u
        out[1, x] = out[1, x] - along * d_u + damp_v * d_p
        out[2, x] = out[2, x] - along * axial(2)
        out[3, x] = out[3, x] - along * axial(3)
        out[4, x] = out[4, x] - along * d_p - DT * d_u

    def own_layers(f, x):
        above = [(a, fx[f, 3 + x + s]) for s, a in taps if x + s <= 7]
        return above + [(-a, fx[f, 3 + x - s]) for s, a in taps if x - s >= 0]

    for x in range(8):
        add_axial(x, own_layers)

    cuts = jnp.concatenate([cut[...]] * 8, axis=1)
    keep = jnp.where(row + 1 <= cuts, 2.0 / (n_ta * gr.shape[1]), 0.0)
    across.wait_recv()

    total = []
    for h, c in ((0, new_a), (1, new_b)):
        parts = [pr[5 * h + i] for i in range(5)]
        tiles = list(parts)
        for first in (80, 96, 112):
            tile = left(parts[0], first)
            for i in range(1, 5):
                tile = jnp.where(lane < 16 * i, tile, left(parts[i], first - 16 * i))
            tiles.append(tile)
        total.append((c + sign * jnp.concatenate(tiles, axis=0)) * keep)
    both = jnp.concatenate(total, axis=0)
    mean_mode = (zero8 + pr[10])[0:1] * (1.0 / (n_ta * gr.shape[1]))
    filtered = jnp.dot(inverse[...], both, precision=highest, preferred_element_type=F32) + mean_mode
    bs[...] = narrow(filtered.reshape(half, -1, LANES), lane)

    b_copies = []
    for i in farthest_first:
        there = lax.rem(k + i, half)
        copy = remote(bs.at[there], br.at[k], b_send.at[i - 1], b_recv.at[i - 1], ta=base + there)
        copy.start()
        b_copies.append(copy)
    br[k] = bs[k]

    pl.when(has_low)(lambda: each(fx_up, "wait_recv"))
    for x in range(3):
        add_axial(x, lambda f, x: [(-a, fx[f, 3 + x - s]) for s, a in taps if x - s < 0])
    pl.when(has_high)(lambda: each(fx_down, "wait_recv"))
    for x in range(5, 8):
        add_axial(x, lambda f, x: [(a, fx[f, 3 + x + s]) for s, a in taps if x + s > 7])

    each(b_copies, "wait_recv")

    def merge(x, carry):
        t = widen(br[x], lane)
        for f in range(5):
            out[f, x] = jnp.where(lane < NF, left(t, 16 * f) if f else t, out[f, x])
        return carry

    lax.fori_loop(0, 8, merge, 0, unroll=4)

    pl.when(has_high)(lambda: each(h_up, "wait_send"))
    pl.when(has_low)(lambda: each(h_down, "wait_send"))
    pl.when(has_high)(lambda: each(fx_up, "wait_send"))
    pl.when(has_low)(lambda: each(fx_down, "wait_send"))
    each(a_copies + [across] + b_copies + [th_down, th_up], "wait_send")


def tables(points, n_theta):
    n = np.arange(points)
    m = np.arange(1, MODES + 1)
    phase = (m[:, None] * n[None, :] % n_theta) * (2.0 * math.pi / n_theta)
    forward = np.concatenate([np.cos(phase), np.sin(phase)]).astype(np.float32)
    return forward, np.ascontiguousarray(forward.T)


def solution(mesh):
    n_gx, n_ta = mesh.shape["gx"], mesh.shape["ta"]

    def on_device(fields, mean_axial, cycle_mean_density, pml_layer, cycle_cutoff):
        nf, nx, nt, nr = fields.shape
        n_theta = nt * n_ta
        forward, inverse = tables(n_theta // 2, n_theta)
        vmem = pl.BlockSpec(memory_space=pltpu.VMEM)
        half = n_ta // 2
        dma = pltpu.SemaphoreType.DMA
        return pl.pallas_call(
            functools.partial(body, n_gx, n_ta, RUN, 2.0 * math.pi / n_theta),
            out_shape=pltpu.VMEM(fields.shape, F32),
            in_specs=[pl.BlockSpec(memory_space=pltpu.HBM)] * 7,
            out_specs=vmem,
            scratch_shapes=[
                pltpu.VMEM((nx, nr), F32),
                pltpu.VMEM((1, nr), F32),
                pltpu.VMEM((nx, nr), jnp.int32),
                pltpu.VMEM((1, NF), jnp.int32),
                pltpu.VMEM(forward.shape, F32),
                pltpu.VMEM(inverse.shape, F32),
                dma((6,)),
                pltpu.VMEM((nf, nx + 6, nt, nr), F32),
                pltpu.VMEM((2, nx, nt + 16, nr), F32),
                pltpu.VMEM((nx + 6, nt, nr), F32),
                pltpu.VMEM((nx, nt, nr), F32),
                pltpu.VMEM((nx, nt, nr), F32),
                pltpu.VMEM((nx, nt, nr), F32),
                pltpu.VMEM((nx, nt, nr), F32),
                pltpu.VMEM((nx, nt, nr), F32),
                pltpu.VMEM((6, nt - 8, nr), F32),
                pltpu.VMEM((2, half, nt - 8, nr), F32),
                pltpu.VMEM((2, nx, 8, nr), F32),
                pltpu.VMEM((2, nx, 8, nr), F32),
                pltpu.VMEM((11, 8, nr), F32),
                pltpu.VMEM((11, 8, nr), F32),
                pltpu.VMEM((nx, nt - 8, nr), F32),
                pltpu.VMEM((nx, nt - 8, nr), F32),
                pltpu.VMEM((nx, nr), F32),
                pltpu.VMEM((nx, nr), F32),
                pltpu.VMEM((nx, nr), F32),
                dma((6,)),
                dma((2, 2)), dma((2, 2)),
                dma((2,)), dma((2,)),
                dma((6,)), dma((2, half)),
                dma((half - 1,)), dma((half - 1,)),
                dma, dma,
                dma((half - 1,)), dma((half - 1,)),
                pltpu.SemaphoreType.REGULAR,
            ],
            compiler_params=pltpu.CompilerParams(
                collective_id=0, has_side_effects=True, vmem_limit_bytes=40 * 1024 * 1024
            ),
        )(*[pltpu.with_memory_space_constraint(a, pltpu.HBM) for a in (
            fields,
            mean_axial,
            cycle_mean_density.reshape(1, nr),
            pml_layer,
            cycle_cutoff.reshape(1, NF),
            jnp.asarray(forward),
            jnp.asarray(inverse),
        )])

    return jax.shard_map(
        on_device,
        mesh=mesh,
        in_specs=(P(None, "gx", "ta", None), P("gx", None), P(), P("gx", None), P()),
        out_specs=P(None, "gx", "ta", None),
        check_vma=False,
    )
```
